512 devices in a mesh: group: 16 (over y, z_lo), rows: 4 (over z_hi), tensor: 8 (over x, core).
Axes of the slice: x: 4, y: 4, z: 16 (z_hi: 4, z_lo: 4; z = z_hi * 4 + z_lo), core: 2. Of those that a mesh axis runs over, the one named last changes fastest.
Arguments:
- continuation_query: bfloat16 [2048, 4, 8192], P(('group', 'rows'), None, 'tensor'), may hold values from -24 to 24
- continuation_keys: bfloat16 [2048, 4, 1024], P(('group', 'rows'), None, 'tensor'), may hold values from -4 to 4
- continuation_values: bfloat16 [2048, 4, 1024], P(('group', 'rows'), None, 'tensor'), may hold values from -4 to 4
- prefix_cache_keys: bfloat16 [16, 1024, 1024], P('group', 'rows', 'tensor'), may hold values from -9.5 to 9.5
- prefix_cache_values: bfloat16 [16, 1024, 1024], P('group', 'rows', 'tensor'), may hold values from -4 to 4
- prefix_block_index: int32 [2048, 1], P('group'), may hold values from 0 to 15; in each aligned block of 32 rows (0 to 31, 32 to 63, ...) at most 4 rows name the same one
- prefix_lens: int32 [16], replicated, may hold values from 256 to 1024, as said below
- out_weight: bfloat16 [8192, 8192], P('tensor', 'rows'), may hold values from -1.1953125 to 1.1953125
Outputs:
- projected: bfloat16 [2048, 4, 8192], P('group', None, ('rows', 'tensor'))
The draws below stay inside these ranges and needn't reach their ends.
Inputs may be any that keep to these rules, and one draw needn't show every extreme that they name: `prefix_lens`: one prefix block in every draw has all 1024 positions valid. `prefix_block_index`: among the 32 rows of one device no prefix block is read by more than 4 rows, and some device has one read by exactly 4.
All inputs are finite; a program needn't handle non-finite values.
Results may differ from the reference program's by a relative error of at most 0.025.
Values may be sent and summed in bfloat16 or wider, within the bound.
A program may use at most 64 MiB of HBM per device.

```python
import math
import jax
import jax.numpy as jnp
import numpy as np
from jax import lax

D = 8192
QUERY_HEADS = 64
KEY_VALUE_HEADS = 8
HEAD_DIMENSION = 128
PREFIX_LENGTH = 1024
RD = 32
ROW_POSITIONS = 4
PREFIX_COUNT = 16
TOTAL_ROWS = 2048
CAP = 4


def draw_continuation_query(key, part):
    key = jax.random.fold_in(key, 1)
    return jax.random.truncated_normal(key, -4.0, 4.0, (TOTAL_ROWS, ROW_POSITIONS, QUERY_HEADS * HEAD_DIMENSION), jnp.float32).astype(jnp.bfloat16)


def draw_prefix_cache_keys(key, part):
    key = jax.random.fold_in(key, 2)
    return jax.random.truncated_normal(key, -4.0, 4.0, (PREFIX_COUNT, PREFIX_LENGTH, KEY_VALUE_HEADS * HEAD_DIMENSION), jnp.float32).astype(jnp.bfloat16)


def draw_prefix_lens(key, part):
    key = jax.random.fold_in(key, 3)
    lengths = jax.random.randint(key, (PREFIX_COUNT,), PREFIX_LENGTH // 4, PREFIX_LENGTH + 1, jnp.int32)
    full_one = jax.random.randint(jax.random.fold_in(key, 4), (), 0, PREFIX_COUNT, jnp.int32)
    return lengths.at[full_one].set(PREFIX_LENGTH)


def block_scale(rng, shape, split, smallest, high):
    gain, own = 1.0, jax.random.fold_in(rng, 6)
    for dim, blocks in split:
        draws = jnp.exp(jax.random.uniform(jax.random.fold_in(own, dim), (blocks,), jnp.float32, smallest / len(split), high / len(split)))
        gain = gain * jnp.repeat(draws, shape[dim] // blocks).reshape([-1 if axis == dim else 1 for axis in range(len(shape))])
    return gain


def shared_out(key, own, number, rows, amount, top, bound, slope):
    ranking = jax.random.permutation(key, amount)
    crowded, ordinary = load_shares(amount, rows * top, bound, slope, True), load_shares(amount, rows * top, bound, slope, False)
    places = jnp.arange(amount)

    def named(sizes, rotation):
        used = int((sizes > 0).sum())
        fixed = max(1, used // 4)
        passed = fixed + (places - fixed + rotation * (used - fixed)) % max(1, amount - fixed)
        return jnp.zeros((amount,), jnp.int32).at[ranking[jnp.where(places < fixed, places, passed)]].set(jnp.asarray(sizes, jnp.int32))

    sizes = jnp.where(number % 4 == 0, named(crowded, number // 4), named(ordinary, number - number // 4 - 1))
    mixed = jax.random.permutation(jax.random.fold_in(own, 3), amount)
    source_of, sink = mixed[0:amount // 2 * 2:2], mixed[1:amount // 2 * 2:2]
    margin = jnp.minimum(sizes[source_of] - 1, bound - sizes[sink]) // 2
    margin = jnp.where((source_of == ranking[0]) | (sink == ranking[0]) | (sizes[sink] == 0), 0, jnp.maximum(margin, 0))
    passed = jax.random.randint(jax.random.fold_in(own, 4), (amount // 2,), 0, 1 << 20) % (margin + 1)
    sizes = sizes.at[source_of].add(-passed).at[sink].add(passed)
    members = jnp.searchsorted(jnp.cumsum(sizes), jnp.arange(rows * top), side="right").astype(jnp.int32)
    grid = members.reshape(top, rows).T
    grid = grid[jax.random.permutation(jax.random.fold_in(own, 1), rows)]
    rotation = jax.random.randint(jax.random.fold_in(own, 2), (rows, 1), 0, top)
    return jnp.take_along_axis(grid, (jnp.arange(top)[None, :] + rotation) % top, axis=1)


def load_shares(amount, total, most, lean, full):
    portions = [(1 << 20) // math.isqrt(standing ** lean) + 1 for standing in range(1, amount + 1)]
    largest = most if full else min(most, max(-(-total // amount), total * portions[0] // sum(portions)))
    least = 1 if total - largest >= amount - 1 else 0
    given, rest = [largest] + [least] * (amount - 1), total - largest - least * (amount - 1)
    while rest > 0:
        free = [i for i in range(1, amount) if given[i] < largest] or [i for i in range(1, amount) if given[i] < most]
        mass, budget = sum([portions[i] for i in free]), rest
        for i in free:
            extra = min(most - given[i], max(1, budget * portions[i] // mass), rest)
            given[i] = given[i] + extra
            rest = rest - extra
    return np.array(given)


def normal_values(own_key, shape, deviation, bound, shards=(), kind=jnp.bfloat16):
    factor_of = block_scale(own_key, shape, shards, -0.22, 0.18) if shards else 1.0
    entries = jax.random.normal(own_key, shape, jnp.float32) * deviation * factor_of
    return jnp.minimum(jnp.maximum(entries, -bound), bound).astype(kind)


def setup_inputs(seed: int = 0) -> dict:
    keys = jax.random.split(jax.random.key(seed), 9)
    continuation_query = draw_continuation_query(jax.random.fold_in(keys[8], 71), 0)
    continuation_keys = normal_values(keys[1], (TOTAL_ROWS, ROW_POSITIONS, KEY_VALUE_HEADS * HEAD_DIMENSION), 1.0, 4.0, ((0, 64), (2, 8)))
    continuation_values = normal_values(keys[2], (TOTAL_ROWS, ROW_POSITIONS, KEY_VALUE_HEADS * HEAD_DIMENSION), 1.0, 4.0, ((0, 64), (2, 8)))
    prefix_cache_keys = draw_prefix_cache_keys(jax.random.fold_in(keys[8], 71), 0)
    prefix_cache_values = normal_values(keys[4], (PREFIX_COUNT, PREFIX_LENGTH, KEY_VALUE_HEADS * HEAD_DIMENSION), 1.0, 4.0, ((0, 16), (1, 4), (2, 8)))
    prefix_block_index_keys = jax.random.split(jax.random.fold_in(keys[5], 1), TOTAL_ROWS // RD)
    prefix_block_index_turns = jax.random.permutation(jax.random.fold_in(keys[5], 3), TOTAL_ROWS // RD)
    prefix_block_index = jax.vmap(lambda own, number: shared_out(jax.random.fold_in(keys[5], 2), own, number, RD, PREFIX_COUNT, 1, CAP, 0))(prefix_block_index_keys, prefix_block_index_turns).reshape((TOTAL_ROWS, 1))
    prefix_lens = draw_prefix_lens(jax.random.fold_in(keys[8], 71), 0)
    out_weight = normal_values(keys[7], (QUERY_HEADS * HEAD_DIMENSION, D), 0.2, 1.1953125, ((0, 8), (1, 4)))
    return dict(continuation_query=continuation_query, continuation_keys=continuation_keys, continuation_values=continuation_values, prefix_cache_keys=prefix_cache_keys, prefix_cache_values=prefix_cache_values, prefix_block_index=prefix_block_index, prefix_lens=prefix_lens, out_weight=out_weight)


floor_score = -1e+30

def attend_block(query_matrix, self_keys, self_values, row_numbers, prefix_cache_keys, prefix_cache_values, prefix_lens):
    row_count_total = query_matrix.shape[0]
    query_groups = QUERY_HEADS // KEY_VALUE_HEADS
    scale_factor = 1.0 / math.sqrt(HEAD_DIMENSION)
    reshaped_query = query_matrix.astype(jnp.float32).reshape(row_count_total, ROW_POSITIONS, KEY_VALUE_HEADS, query_groups, HEAD_DIMENSION)
    selected_keys = jnp.take(prefix_cache_keys, row_numbers, axis=0).astype(jnp.float32).reshape(row_count_total, PREFIX_LENGTH, KEY_VALUE_HEADS, HEAD_DIMENSION)
    selected_values = jnp.take(prefix_cache_values, row_numbers, axis=0).astype(jnp.float32).reshape(row_count_total, PREFIX_LENGTH, KEY_VALUE_HEADS, HEAD_DIMENSION)
    reshaped_keys = self_keys.astype(jnp.float32).reshape(row_count_total, ROW_POSITIONS, KEY_VALUE_HEADS, HEAD_DIMENSION)
    reshaped_values = self_values.astype(jnp.float32).reshape(row_count_total, ROW_POSITIONS, KEY_VALUE_HEADS, HEAD_DIMENSION)
    prefix_scores = jnp.einsum('bshgd,bphd->bhgsp', reshaped_query, selected_keys) * scale_factor
    positions = jnp.arange(PREFIX_LENGTH, dtype=jnp.int32)
    usable = positions[None, :] < jnp.take(prefix_lens, row_numbers)[:, None]
    usable = usable[:, None, None, None, :]
    prefix_scores = jnp.where(usable, prefix_scores, floor_score)
    own_scores = jnp.einsum('bshgd,bthd->bhgst', reshaped_query, reshaped_keys) * scale_factor
    causal = jnp.arange(ROW_POSITIONS)[None, :] <= jnp.arange(ROW_POSITIONS)[:, None]
    own_scores = jnp.where(causal, own_scores, floor_score)
    peak = jnp.maximum(prefix_scores.max(-1), own_scores.max(-1))
    prefix_weights = jnp.where(usable, jnp.exp(prefix_scores - peak[..., None]), 0.0)
    own_weights = jnp.where(causal, jnp.exp(own_scores - peak[..., None]), 0.0)
    total = prefix_weights.sum(-1) + own_weights.sum(-1)
    rounded_prefix = lax.optimization_barrier(prefix_weights.astype(jnp.bfloat16)).astype(jnp.float32)
    rounded_own = lax.optimization_barrier(own_weights.astype(jnp.bfloat16)).astype(jnp.float32)
    summed = jnp.einsum('bhgsp,bphd->bhgsd', rounded_prefix, selected_values)
    summed = summed + jnp.einsum('bhgst,bthd->bhgsd', rounded_own, reshaped_values)
    normalized = summed / total[..., None]
    normalized = normalized.transpose(0, 3, 1, 2, 4).reshape(row_count_total, ROW_POSITIONS, QUERY_HEADS * HEAD_DIMENSION)
    return normalized.astype(jnp.bfloat16)

def reference(continuation_query, continuation_keys, continuation_values, prefix_cache_keys, prefix_cache_values, prefix_block_index, prefix_lens, out_weight):
    block_of_rows = math.gcd(TOTAL_ROWS, 32)
    count_of_blocks = TOTAL_ROWS // block_of_rows

    def one_block(items):
        return attend_block(items[0], items[1], items[2], items[3], prefix_cache_keys, prefix_cache_values, prefix_lens)
    stacked_tensors = (continuation_query.reshape(count_of_blocks, block_of_rows, ROW_POSITIONS, QUERY_HEADS * HEAD_DIMENSION), continuation_keys.reshape(count_of_blocks, block_of_rows, ROW_POSITIONS, KEY_VALUE_HEADS * HEAD_DIMENSION), continuation_values.reshape(count_of_blocks, block_of_rows, ROW_POSITIONS, KEY_VALUE_HEADS * HEAD_DIMENSION), prefix_block_index.reshape(count_of_blocks, block_of_rows))
    attended = lax.map(one_block, stacked_tensors).reshape(TOTAL_ROWS * ROW_POSITIONS, QUERY_HEADS * HEAD_DIMENSION)
    projected = jnp.dot(attended, out_weight, preferred_element_type=jnp.float32)
    return projected.reshape(TOTAL_ROWS, ROW_POSITIONS, D).astype(jnp.bfloat16)
```

```python
import functools
import math

import jax
import jax.numpy as jnp
from jax import lax
from jax.experimental import pallas as pl
from jax.experimental.pallas import tpu as pltpu
from jax.sharding import PartitionSpec as P

MESH = pl.DeviceIdType.MESH
SCALE = 1.0 / math.sqrt(128.0)
F32 = jnp.float32
BF16 = jnp.bfloat16
RP = 4
AP = 4


def place():
    g = lax.axis_index("group")
    return g // 4, lax.axis_index("rows") * 4 + lax.rem(g, 4), lax.axis_index("tensor")


def device(y, z, t):
    y, z, t = lax.rem(y + 4, 4), lax.rem(z + 16, 16), lax.rem(t + 8, 8)
    return (y * 4 + lax.rem(z, 4), z // 4, t)


def dot(a, b, da, db):
    return lax.dot_general(a, b, (((da,), (db,)), ((), ())), preferred_element_type=F32)


def kernel(
    q_hbm, ck_hbm, cv_hbm, pk_hbm, pv_hbm, idx_hbm, lens, w_hbm, out_ref,
    q_in, ck_in, cv_in, pv_in, idx_in, w, kk, vt, qs, rq, qb, top, tot, acc, rs, rr, oht, att, ps, pr,
    load_sem, ring_s, ring_r, q_s, q_r, ret_s, ret_r, ag_s, ag_r, p_s, p_r,
):
    y, z, t = place()
    z_lo, h = lax.rem(z, 4), z // 4

    loads = []
    for n, (src, dst) in enumerate(
        (
            (pk_hbm.at[0], kk.at[0]),
            (pv_hbm.at[0], pv_in),
            (idx_hbm, idx_in),
            (q_hbm, q_in),
            (ck_hbm, ck_in),
            (cv_hbm, cv_in),
            (w_hbm, w),
        )
    ):
        loads.append(pltpu.make_async_copy(src, dst, load_sem.at[n]))
        loads[-1].start()

    barrier = pltpu.get_barrier_semaphore()
    partners = [device(y, z + d, t) for d in (1, -1, 4, -4)]
    partners += [device(y + d, z, t) for d in (1, 2, 3)]
    partners += [device(y, z, t + d) for d in range(1, 8)]
    for who in partners:
        pl.semaphore_signal(barrier, inc=1, device_id=who, device_id_type=MESH)

    def remote(src, dst, send, recv, who):
        return pltpu.make_async_remote_copy(
            src_ref=src, dst_ref=dst, send_sem=send, recv_sem=recv, device_id=who, device_id_type=MESH
        )

    def ring(way, piece, d):
        if way == 0:
            a, b, who = d - 1, d, device(y, z + 1, t)
        else:
            a, b, who = lax.rem(17 - d, 16), 16 - d, device(y, z - 1, t)
        buf, part = (kk, pl.ds(128 * piece, 128)) if piece < 2 else (vt, pl.ds(64 * (piece - 2), 64))
        return remote(buf.at[a, part], buf.at[b, part], ring_s.at[way, piece, d], ring_r.at[way, piece, d], who)

    loads[1].wait()
    vt[0] = jnp.transpose(pv_in[...].astype(F32)).astype(BF16)

    loads[2].wait()
    col = jnp.transpose(jnp.broadcast_to(idx_in[...].astype(F32), (128, 128)))
    i = lax.broadcasted_iota(jnp.int32, (128, 128), 0) - h * 32
    row = lax.broadcasted_iota(jnp.int32, (128, 128), 1) // 4
    mine = jnp.sum(jnp.where(i == row, col, 0.0), axis=0, keepdims=True)
    rank = jnp.sum(jnp.where((col == mine) & (i >= 0) & (i < row), 1.0, 0.0), axis=0, keepdims=True)
    position = lax.rem(lax.broadcasted_iota(jnp.int32, (1, 128), 1), 4).astype(F32)
    slot_row = mine * 16.0 + rank * 4.0 + position
    one_hot = jnp.where(lax.broadcasted_iota(jnp.int32, (256, 128), 0).astype(F32) == slot_row, 1.0, 0.0)
    oht[...] = jnp.transpose(one_hot).astype(BF16)
    one_hot = one_hot.astype(BF16)

    for n in (0, 3, 4, 5):
        loads[n].wait()
    pl.semaphore_wait(barrier, len(partners))
    for piece in range(RP):
        for way in range(2):
            ring(way, piece, 1).start()

    def rows_of(ref):
        return ref[...].astype(F32).reshape(128, ref.shape[2]).astype(BF16)

    qs[:, :, 0:1024] = dot(one_hot, rows_of(q_in), 1, 0).astype(BF16).reshape(4, 64, 1024)
    qs[:, :, 1024:1152] = dot(one_hot, rows_of(ck_in), 1, 0).astype(BF16).reshape(4, 64, 128)
    qs[:, :, 1152:1280] = dot(one_hot, rows_of(cv_in), 1, 0).astype(BF16).reshape(4, 64, 128)
    q_copies = []
    for d in (1, 2, 3):
        q_copies.append(
            remote(qs.at[lax.rem(y + d, 4)], rq.at[y], q_s.at[d], q_r.at[d], device(y + d, z, t))
        )
        q_copies[-1].start()
    rq[y] = qs[y]
    for copy in q_copies:
        copy.wait_recv()

    def begin(rel, _):
        at = pl.ds(pl.multiple_of(lax.rem(z_lo + rel, 4) * 16, 16), 16)
        for g in range(8):
            for source in range(4):
                qb[rel, pl.ds(g * 64 + source * 16, 16), :] = rq[source, at, g * 128 : (g + 1) * 128]
        keys = jnp.concatenate([rq[source, at, 1024:1152] for source in range(4)], axis=0)
        values = jnp.concatenate([rq[source, at, 1152:1280] for source in range(4)], axis=0)
        s = dot(keys, qb[rel], 1, 1)
        key_row = lax.broadcasted_iota(jnp.int32, (64, 512), 0)
        query_row = lax.rem(lax.broadcasted_iota(jnp.int32, (64, 512), 1), 64)
        seen = (key_row // 4 == query_row // 4) & (key_row <= query_row)
        s = jnp.where(seen, s, -1e30)
        peak = jnp.max(s, axis=0, keepdims=True)
        e = jnp.exp((s - peak) * SCALE)
        top[rel] = peak
        tot[rel] = jnp.sum(e, axis=0, keepdims=True)
        acc[rel] = dot(values, e.astype(BF16), 0, 0)
        return 0

    lax.fori_loop(0, 4, begin, 0)

    def attend(k):
        rel = lax.rem(16 - k, 4)
        source = lax.rem(z - k + 16, 16)
        valid = lens[y * 4 + lax.rem(source, 4)] - 256 * (source // 4)
        s = dot(kk[k], qb[rel], 1, 1)
        s = jnp.where(lax.broadcasted_iota(jnp.int32, (256, 512), 0) < valid, s, -1e30)
        before = top[rel]
        peak = jnp.maximum(before, jnp.max(s, axis=0, keepdims=True))
        e = jnp.exp((s - peak) * SCALE)
        fade = jnp.exp((before - peak) * SCALE)
        top[rel] = peak
        tot[rel] = tot[rel] * fade + jnp.sum(e, axis=0, keepdims=True)
        acc[rel] = acc[rel] * fade + dot(vt[k], e.astype(BF16), 1, 0)

    attend(0)

    def step(d, _):
        for piece in range(RP):
            for way in range(2):
                ring(way, piece, d).wait_recv()
                if (piece < 2) == (way == 0):
                    ring(way, piece, d + 1).start()
                else:
                    pl.when(d < 7)(ring(way, piece, d + 1).start)

        def both(j, _):
            attend(jnp.where(j == 0, d, 16 - d))
            return 0

        lax.fori_loop(0, 2, both, 0)
        return 0

    lax.fori_loop(1, 8, step, 0)

    def hand_back(d, rel, at):
        return remote(
            rs.at[lax.rem(y + d, 4), at], rr.at[y, at], ret_s.at[d, rel], ret_r.at[d, rel], device(y + d, z, t)
        )

    def slot_rows(rel):
        return pl.ds(pl.multiple_of(lax.rem(z_lo + rel, 4) * 16, 16), 16)

    def finish(rel, _):
        at = slot_rows(rel)
        o = jnp.transpose(acc[rel] / tot[rel]).astype(BF16)
        for source in range(4):
            for g in range(8):
                lo = g * 64 + source * 16
                rs[source, at, g * 128 : (g + 1) * 128] = o[lo : lo + 16, :]
        for d in (1, 2, 3):
            hand_back(d, rel, at).start()
        rr[y, at, :] = rs[y, at, :]
        return 0

    lax.fori_loop(1, 4, finish, 0)
    for piece in range(RP):
        ring(0 if piece < 2 else 1, piece, 8).wait_recv()
    attend(8)
    finish(0, 0)
    for rel in range(4):
        for d in (1, 2, 3):
            hand_back(d, rel, slot_rows(rel)).wait_recv()

    att[0] = dot(oht[...], rr[...].reshape(256, 1024), 1, 0).astype(BF16)

    def spread(way, piece):
        up, rows = way % 2 == 0, 128 // AP
        if way < 2:
            src, dst, part = 0, 1 if up else 3, pl.ds(piece * rows, rows)
        else:
            src, dst = 1 if up else 3, 2
            part = pl.ds(piece * rows + (0 if up else rows // 2), rows // 2)
        who = device(y, z + 4 if up else z - 4, t)
        return remote(att.at[src, part], att.at[dst, part], ag_s.at[way, piece], ag_r.at[way, piece], who)

    for piece in range(AP):
        for way in range(2):
            spread(way, piece).start()

    loads[6].wait()

    def share(d, number, at):
        return remote(ps.at[d, at], pr.at[d, at], p_s.at[number, d], p_r.at[number, d], device(y, z, t + d))

    def project(a, number, at):
        def column(d, _):
            cols = pl.ds(pl.multiple_of(lax.rem(t + d, 8) * 256, 256), 256)
            part = dot(a, w[:, cols], 1, 0).astype(BF16)

            @pl.when(d < 8)
            def _():
                ps[d, at, :] = part
                share(d, number, at).start()

            @pl.when(d == 8)
            def _():
                pr[0, at, :] = part

            return 0

        lax.fori_loop(1, 9, column, 0)

    spans = [pl.ds(0, 128)]
    project(att[0], 0, spans[0])
    rows = 128 // AP
    for piece in range(AP):
        for way in range(2):
            spread(way, piece).wait_recv()
            spread(way + 2, piece).start()
        spans.append(pl.ds(128 + piece * 2 * rows, 2 * rows))
        lo = piece * rows
        project(jnp.concatenate([att[1, lo : lo + rows], att[3, lo : lo + rows]], axis=0), 1 + piece, spans[-1])
    for piece in range(AP):
        for way in range(2):
            spread(way + 2, piece).wait_recv()
        spans.append(pl.ds(384 + piece * rows, rows))
        project(att[2, piece * rows : (piece + 1) * rows], 1 + AP + piece, spans[-1])

    def result(number, at, pieces):
        for d in range(1, 8):
            share(d, number, at).wait_recv()
        total = pr[0, at, :].astype(F32)
        for d in range(1, 8):
            total = total + pr[d, at, :].astype(F32)
        for below, lo, first, count in pieces:
            home = lax.rem(h - below + 4, 4) * 32 + first // 4
            part = total[lo : lo + count].reshape(count // 4, 4, 256)
            out_ref[pl.ds(home, count // 4)] = part.astype(BF16)

    result(0, spans[0], [(0, 0, 0, 128)])
    for piece in range(AP):
        result(1 + piece, spans[1 + piece], [(1, 0, piece * rows, rows), (3, rows, piece * rows, rows)])
    for piece in range(AP):
        result(1 + AP + piece, spans[1 + AP + piece], [(2, 0, piece * rows, rows)])

    def sent(d, _):
        for piece in range(RP):
            for way in range(2):
                if (piece < 2) == (way == 0):
                    ring(way, piece, d).wait_send()
                else:
                    pl.when(d < 8)(ring(way, piece, d).wait_send)
        return 0

    lax.fori_loop(1, 9, sent, 0)
    for copy in q_copies:
        copy.wait_send()
    for rel in range(4):
        for d in (1, 2, 3):
            hand_back(d, rel, slot_rows(rel)).wait_send()
    for piece in range(AP):
        for way in range(4):
            spread(way, piece).wait_send()
    for number, at in enumerate(spans):
        for d in range(1, 8):
            share(d, number, at).wait_send()


def local(q, ck, cv, pk, pv, index, lens, w):
    dma = pltpu.SemaphoreType.DMA
    anywhere = pl.BlockSpec(memory_space=pl.ANY)
    return pl.pallas_call(
        kernel,
        out_shape=jax.ShapeDtypeStruct((128, 4, 256), BF16),
        in_specs=[anywhere] * 6 + [pl.BlockSpec(memory_space=pltpu.SMEM), anywhere],
        out_specs=pl.BlockSpec(memory_space=pltpu.VMEM),
        scratch_shapes=[
            pltpu.VMEM((32, 4, 1024), BF16),
            pltpu.VMEM((32, 4, 128), BF16),
            pltpu.VMEM((32, 4, 128), BF16),
            pltpu.VMEM((256, 128), BF16),
            pltpu.VMEM((1, 128), jnp.int32),
            pltpu.VMEM((1024, 2048), BF16),
            pltpu.VMEM((16, 256, 128), BF16),
            pltpu.VMEM((16, 128, 256), BF16),
            pltpu.VMEM((4, 64, 1280), BF16),
            pltpu.VMEM((4, 64, 1280), BF16),
            pltpu.VMEM((4, 512, 128), BF16),
            pltpu.VMEM((4, 1, 512), F32),
            pltpu.VMEM((4, 1, 512), F32),
            pltpu.VMEM((4, 128, 512), F32),
            pltpu.VMEM((4, 64, 1024), BF16),
            pltpu.VMEM((4, 64, 1024), BF16),
            pltpu.VMEM((128, 256), BF16),
            pltpu.VMEM((4, 128, 1024), BF16),
            pltpu.VMEM((8, 512, 256), BF16),
            pltpu.VMEM((8, 512, 256), BF16),
            dma((7,)),
            dma((2, RP, 9)),
            dma((2, RP, 9)),
            dma((4,)),
            dma((4,)),
            dma((4, 4)),
            dma((4, 4)),
            dma((4, AP)),
            dma((4, AP)),
            dma((1 + 2 * AP, 8)),
            dma((1 + 2 * AP, 8)),
        ],
        compiler_params=pltpu.CompilerParams(
            collective_id=0, has_side_effects=True, vmem_limit_bytes=48 * 1024 * 1024
        ),
    )(q, ck, cv, pk, pv, index.reshape(1, 128), lens, w)


def solution(mesh):
    return jax.shard_map(
        local,
        mesh=mesh,
        in_specs=(
            P(("group", "rows"), None, "tensor"),
            P(("group", "rows"), None, "tensor"),
            P(("group", "rows"), None, "tensor"),
            P("group", "rows", "tensor"),
            P("group", "rows", "tensor"),
            P("group", None),
            P(),
            P("tensor", "rows"),
        ),
        out_specs=P("group", None, ("rows", "tensor")),
        check_vma=False,
    )
```

```python
import functools
import math

import jax
import jax.numpy as jnp
from jax import lax
from jax.experimental import pallas as pl
from jax.experimental.pallas import tpu as pltpu
from jax.sharding import PartitionSpec as P

MESH = pl.DeviceIdType.MESH
SCALE = 1.0 / math.sqrt(128.0)
F32 = jnp.float32
BF16 = jnp.bfloat16
RP = 4
AP = 4


def place():
    g = lax.axis_index("group")
    return g // 4, lax.axis_index("rows") * 4 + lax.rem(g, 4), lax.axis_index("tensor")


def device(y, z, t):
    y, z, t = lax.rem(y + 4, 4), lax.rem(z + 16, 16), lax.rem(t + 8, 8)
    return (y * 4 + lax.rem(z, 4), z // 4, t)


def dot(a, b, da, db):
    return lax.dot_general(a, b, (((da,), (db,)), ((), ())), preferred_element_type=F32)


def kernel(
    q_hbm, ck_hbm, cv_hbm, pk_hbm, pv_hbm, idx_hbm, lens, w_hbm, out_ref,
    q_in, ck_in, cv_in, pv_in, idx_in, w, kk, vt, qs, rq, qb, top, tot, acc, rs, rr, oht, att, ps, pr,
    load_sem, ring_s, ring_r, q_s, q_r, ret_s, ret_r, ag_s, ag_r, p_s, p_r,
):
    y, z, t = place()
    z_lo, h = lax.rem(z, 4), z // 4

    loads = []
    for n, (src, dst) in enumerate(
        (
            (pk_hbm.at[0], kk.at[0]),
            (pv_hbm.at[0], pv_in),
            (idx_hbm, idx_in),
            (q_hbm, q_in),
            (ck_hbm, ck_in),
            (cv_hbm, cv_in),
            (w_hbm, w),
        )
    ):
        loads.append(pltpu.make_async_copy(src, dst, load_sem.at[n]))
        loads[-1].start()

    barrier = pltpu.get_barrier_semaphore()
    partners = [device(y, z + d, t) for d in (1, -1, 4, -4)]
    partners += [device(y + d, z, t) for d in (1, 2, 3)]
    partners += [device(y, z, t + d) for d in range(1, 8)]
    for who in partners:
        pl.semaphore_signal(barrier, inc=1, device_id=who, device_id_type=MESH)

    def remote(src, dst, send, recv, who):
        return pltpu.make_async_remote_copy(
            src_ref=src, dst_ref=dst, send_sem=send, recv_sem=recv, device_id=who, device_id_type=MESH
        )

    def ring(way, piece, d):
        if way == 0:
            a, b, who = d - 1, d, device(y, z + 1, t)
        else:
            a, b, who = lax.rem(17 - d, 16), 16 - d, device(y, z - 1, t)
        n = piece % (RP // 2)
        if piece < RP // 2:
            buf, part = kk, pl.ds(n * (512 // RP), 512 // RP)
        else:
            buf, part = vt, pl.ds(n * (256 // RP), 256 // RP)
        return remote(buf.at[a, part], buf.at[b, part], ring_s.at[piece // (RP // 2)], ring_r.at[way, piece, d], who)

    loads[1].wait()
    vt[0] = jnp.transpose(pv_in[...].astype(F32)).astype(BF16)

    loads[2].wait()
    col = jnp.transpose(jnp.broadcast_to(idx_in[...].astype(F32), (128, 128)))
    i = lax.broadcasted_iota(jnp.int32, (128, 128), 0) - h * 32
    row = lax.broadcasted_iota(jnp.int32, (128, 128), 1) // 4
    mine = jnp.sum(jnp.where(i == row, col, 0.0), axis=0, keepdims=True)
    rank = jnp.sum(jnp.where((col == mine) & (i >= 0) & (i < row), 1.0, 0.0), axis=0, keepdims=True)
    position = lax.rem(lax.broadcasted_iota(jnp.int32, (1, 128), 1), 4).astype(F32)
    slot_row = mine * 16.0 + rank * 4.0 + position
    one_hot = jnp.where(lax.broadcasted_iota(jnp.int32, (256, 128), 0).astype(F32) == slot_row, 1.0, 0.0)
    oht[...] = jnp.transpose(one_hot).astype(BF16)
    one_hot = one_hot.astype(BF16)

    loads[0].wait()
    pl.semaphore_wait(barrier, len(partners))
    for piece in range(RP):
        for way in range(2):
            ring(way, piece, 1).start()
    for n in (3, 4, 5):
        loads[n].wait()

    def rows_of(ref):
        return ref[...].astype(F32).reshape(128, ref.shape[2]).astype(BF16)

    qs[:, :, 0:1024] = dot(one_hot, rows_of(q_in), 1, 0).astype(BF16).reshape(4, 64, 1024)
    qs[:, :, 1024:1152] = dot(one_hot, rows_of(ck_in), 1, 0).astype(BF16).reshape(4, 64, 128)
    qs[:, :, 1152:1280] = dot(one_hot, rows_of(cv_in), 1, 0).astype(BF16).reshape(4, 64, 128)
    q_copies = []
    for d in (1, 2, 3):
        q_copies.append(
            remote(qs.at[lax.rem(y + d, 4)], rq.at[y], q_s.at[0], q_r.at[0], device(y + d, z, t))
        )
        q_copies[-1].start()
    rq[y] = qs[y]

    def begin(rel, _):
        at = pl.ds(pl.multiple_of(lax.rem(z_lo + rel, 4) * 16, 16), 16)
        for g in range(8):
            for source in range(4):
                qb[rel, pl.ds(g * 64 + source * 16, 16), :] = rq[source, at, g * 128 : (g + 1) * 128]
        keys = jnp.concatenate([rq[source, at, 1024:1152] for source in range(4)], axis=0)
        values = jnp.concatenate([rq[source, at, 1152:1280] for source in range(4)], axis=0)
        s = dot(keys, qb[rel], 1, 1)
        key_row = lax.broadcasted_iota(jnp.int32, (64, 512), 0)
        query_row = lax.rem(lax.broadcasted_iota(jnp.int32, (64, 512), 1), 64)
        seen = (key_row // 4 == query_row // 4) & (key_row <= query_row)
        s = jnp.where(seen, s, -1e30)
        peak = jnp.max(s, axis=0, keepdims=True)
        e = jnp.exp((s - peak) * SCALE)
        top[rel] = peak
        tot[rel] = jnp.sum(e, axis=0, keepdims=True)
        acc[rel] = dot(values, e.astype(BF16), 0, 0)
        return 0

    def attend(k):
        rel = lax.rem(16 - k, 4)
        source = lax.rem(z - k + 16, 16)
        valid = lens[y * 4 + lax.rem(source, 4)] - 256 * (source // 4)
        s = dot(kk[k], qb[rel], 1, 1)
        s = jnp.where(lax.broadcasted_iota(jnp.int32, (256, 512), 0) < valid, s, -1e30)
        before = top[rel]
        peak = jnp.maximum(before, jnp.max(s, axis=0, keepdims=True))
        e = jnp.exp((s - peak) * SCALE)
        fade = jnp.exp((before - peak) * SCALE)
        top[rel] = peak
        tot[rel] = tot[rel] * fade + jnp.sum(e, axis=0, keepdims=True)
        acc[rel] = acc[rel] * fade + dot(vt[k], e.astype(BF16), 1, 0)

    def forward(d):
        for piece in range(RP):
            for way in range(2):
                ring(way, piece, d).wait_recv()
                if (piece < RP // 2) == (way == 0):
                    ring(way, piece, d + 1).start()
                else:
                    pl.when(d < 7)(ring(way, piece, d + 1).start)

    def pair(d, _):
        def both(j, _):
            attend(jnp.where(j == 0, d, 16 - d))
            return 0

        return lax.fori_loop(0, 2, both, 0)

    def step(d, _):
        forward(d)
        return pair(d - 2, 0)

    lax.fori_loop(1, 3, lambda d, _: forward(d) or 0, 0)
    remote(rq.at[0:3], rq.at[0:3], q_s.at[0], q_r.at[0], device(y, z, t)).wait_recv()
    lax.fori_loop(0, 4, begin, 0)
    attend(0)
    lax.fori_loop(3, 8, step, 0)
    lax.fori_loop(6, 8, pair, 0)

    def hand_back(d, rel, at):
        return remote(
            rs.at[lax.rem(y + d, 4), at], rr.at[y, at], ret_s.at[0], ret_r.at[rel], device(y + d, z, t)
        )

    def slot_rows(rel):
        return pl.ds(pl.multiple_of(lax.rem(z_lo + rel, 4) * 16, 16), 16)

    def finish(rel, _):
        at = slot_rows(rel)
        o = jnp.transpose(acc[rel] / tot[rel]).astype(BF16)
        for source in range(4):
            for g in range(8):
                lo = g * 64 + source * 16
                rs[source, at, g * 128 : (g + 1) * 128] = o[lo : lo + 16, :]
        for d in (1, 2, 3):
            hand_back(d, rel, at).start()
        rr[y, at, :] = rs[y, at, :]
        return 0

    lax.fori_loop(1, 4, finish, 0)
    for piece in range(RP):
        ring(0 if piece < RP // 2 else 1, piece, 8).wait_recv()
    attend(8)
    finish(0, 0)
    for rel in range(4):
        some = rr.at[0:3, slot_rows(rel)]
        remote(some, some, ret_s.at[0], ret_r.at[rel], device(y, z, t)).wait_recv()

    att[0] = dot(oht[...], rr[...].reshape(256, 1024), 1, 0).astype(BF16)

    def spread(way, piece):
        up, rows = way % 2 == 0, 128 // AP
        if way < 2:
            src, dst, part = 0, 1 if up else 3, pl.ds(piece * rows, rows)
        else:
            src, dst = 1 if up else 3, 2
            part = pl.ds(piece * rows + (0 if up else rows // 2), rows // 2)
        who = device(y, z + 4 if up else z - 4, t)
        return remote(att.at[src, part], att.at[dst, part], ag_s.at[0], ag_r.at[way, piece], who)

    for piece in range(AP):
        for way in range(2):
            spread(way, piece).start()

    loads[6].wait()

    def share(d, number, at):
        return remote(ps.at[d, at], pr.at[d, at], p_s.at[0], p_r.at[number], device(y, z, t + d))

    def project(a, number, at):
        def column(d, _):
            cols = pl.ds(pl.multiple_of(lax.rem(t + d, 8) * 256, 256), 256)
            part = dot(a, w[:, cols], 1, 0).astype(BF16)

            @pl.when(d < 8)
            def _():
                ps[d, at, :] = part
                share(d, number, at).start()

            @pl.when(d == 8)
            def _():
                pr[0, at, :] = part

            return 0

        lax.fori_loop(1, 9, column, 0)

    spans = [pl.ds(0, 128)]
    project(att[0], 0, spans[0])
    rows = 128 // AP
    for piece in range(AP):
        for way in range(2):
            spread(way, piece).wait_recv()
            spread(way + 2, piece).start()
        spans.append(pl.ds(128 + piece * 2 * rows, 2 * rows))
        lo = piece * rows
        project(jnp.concatenate([att[1, lo : lo + rows], att[3, lo : lo + rows]], axis=0), 1 + piece, spans[-1])

    def result(number, at, pieces):
        others = pr.at[1:8, at]
        remote(others, others, p_s.at[0], p_r.at[number], device(y, z, t)).wait_recv()
        total = pr[0, at, :].astype(F32)
        for d in range(1, 8):
            total = total + pr[d, at, :].astype(F32)
        for below, lo, first, count in pieces:
            home = lax.rem(h - below + 4, 4) * 32 + first // 4
            part = total[lo : lo + count].reshape(count // 4, 4, 256)
            out_ref[pl.ds(home, count // 4)] = part.astype(BF16)

    def near(piece):
        result(1 + piece, spans[1 + piece], [(1, 0, piece * rows, rows), (3, rows, piece * rows, rows)])

    def far(piece):
        result(1 + AP + piece, spans[1 + AP + piece], [(2, 0, piece * rows, rows)])

    result(0, spans[0], [(0, 0, 0, 128)])
    for piece in range(AP):
        if piece == AP - 1:
            for n in range(AP):
                near(n)
        for way in range(2):
            spread(way + 2, piece).wait_recv()
        spans.append(pl.ds(384 + piece * rows, rows))
        project(att[2, piece * rows : (piece + 1) * rows], 1 + AP + piece, spans[-1])
    for piece in range(AP):
        far(piece)

    for ref, sem in (
        (kk.at[0:15], ring_s.at[0]),
        (vt.at[0:15], ring_s.at[1]),
        (qs.at[0:3], q_s.at[0]),
        (rs.at[0:3], ret_s.at[0]),
        (att.at[0:3], ag_s.at[0]),
        (ps.at[1:8], p_s.at[0]),
    ):
        remote(ref, ref, sem, p_r.at[0], device(y, z, t)).wait_send()


def local(q, ck, cv, pk, pv, index, lens, w):
    dma = pltpu.SemaphoreType.DMA
    anywhere = pl.BlockSpec(memory_space=pl.ANY)
    return pl.pallas_call(
        kernel,
        out_shape=jax.ShapeDtypeStruct((128, 4, 256), BF16),
        in_specs=[anywhere] * 6 + [pl.BlockSpec(memory_space=pltpu.SMEM), anywhere],
        out_specs=pl.BlockSpec(memory_space=pltpu.VMEM),
        scratch_shapes=[
            pltpu.VMEM((32, 4, 1024), BF16),
            pltpu.VMEM((32, 4, 128), BF16),
            pltpu.VMEM((32, 4, 128), BF16),
            pltpu.VMEM((256, 128), BF16),
            pltpu.VMEM((1, 128), jnp.int32),
            pltpu.VMEM((1024, 2048), BF16),
            pltpu.VMEM((16, 256, 128), BF16),
            pltpu.VMEM((16, 128, 256), BF16),
            pltpu.VMEM((4, 64, 1280), BF16),
            pltpu.VMEM((4, 64, 1280), BF16),
            pltpu.VMEM((4, 512, 128), BF16),
            pltpu.VMEM((4, 1, 512), F32),
            pltpu.VMEM((4, 1, 512), F32),
            pltpu.VMEM((4, 128, 512), F32),
            pltpu.VMEM((4, 64, 1024), BF16),
            pltpu.VMEM((4, 64, 1024), BF16),
            pltpu.VMEM((128, 256), BF16),
            pltpu.VMEM((4, 128, 1024), BF16),
            pltpu.VMEM((8, 512, 256), BF16),
            pltpu.VMEM((8, 512, 256), BF16),
            dma((7,)),
            dma((2,)),
            dma((2, RP, 9)),
            dma((1,)),
            dma((1,)),
            dma((1,)),
            dma((4,)),
            dma((1,)),
            dma((4, AP)),
            dma((1,)),
            dma((1 + 2 * AP,)),
        ],
        compiler_params=pltpu.CompilerParams(
            collective_id=0, has_side_effects=True, vmem_limit_bytes=63 * 1024 * 1024
        ),
    )(q, ck, cv, pk, pv, index.reshape(1, 128), lens, w)


def solution(mesh):
    return jax.shard_map(
        local,
        mesh=mesh,
        in_specs=(
            P(("group", "rows"), None, "tensor"),
            P(("group", "rows"), None, "tensor"),
            P(("group", "rows"), None, "tensor"),
            P("group", "rows", "tensor"),
            P("group", "rows", "tensor"),
            P("group", None),
            P(),
            P("tensor", "rows"),
        ),
        out_specs=P("group", None, ("rows", "tensor")),
        check_vma=False,
    )
```

```python
import functools
import math

import jax
import jax.numpy as jnp
from jax import lax
from jax.experimental import pallas as pl
from jax.experimental.pallas import tpu as pltpu
from jax.sharding import PartitionSpec as P

MESH = pl.DeviceIdType.MESH
SCALE = 1.0 / math.sqrt(128.0)
F32 = jnp.float32
BF16 = jnp.bfloat16
RP = 4
AP = 4


def place():
    g = lax.axis_index("group")
    return g // 4, lax.axis_index("rows") * 4 + lax.rem(g, 4), lax.axis_index("tensor")


def device(y, z, t):
    y, z, t = lax.rem(y + 4, 4), lax.rem(z + 16, 16), lax.rem(t + 8, 8)
    return (y * 4 + lax.rem(z, 4), z // 4, t)


def dot(a, b, da, db):
    return lax.dot_general(a, b, (((da,), (db,)), ((), ())), preferred_element_type=F32)


def kernel(
    q_hbm, ck_hbm, cv_hbm, pk_hbm, pv_hbm, idx_hbm, lens_hbm, w_hbm, out_ref,
    lens, q_in, ck_in, cv_in, pv_in, idx_in, w, kk, vt, qs, rq, qb, top, tot, acc, rs, rr, oht, part_sum, att, ps, pr,
    load_sem, ring_s, ring_r, q_s, q_r, ret_s, ret_r, ag_s, ag_r, p_s, p_r,
):
    y, z, t = place()
    z_lo, h = lax.rem(z, 4), z // 4

    barrier = pltpu.get_barrier_semaphore()
    partners = [device(y, z + d, t) for d in (1, -1, 4, -4)]
    partners += [device(y + d, z, t) for d in (1, 2, 3)]
    partners += [device(y, z, t + d) for d in range(1, 8)]
    for who in partners:
        pl.semaphore_signal(barrier, inc=1, device_id=who, device_id_type=MESH)

    loads = []
    for n, (src, dst) in enumerate(
        (
            (pk_hbm.at[0], kk.at[0]),
            (pv_hbm.at[0], pv_in),
            (idx_hbm, idx_in),
            (q_hbm, q_in),
            (ck_hbm, ck_in),
            (cv_hbm, cv_in),
            (lens_hbm, lens),
            (w_hbm, w),
        )
    ):
        loads.append(pltpu.make_async_copy(src, dst, load_sem.at[n]))
        loads[-1].start()

    def remote(src, dst, send, recv, who):
        return pltpu.make_async_remote_copy(
            src_ref=src, dst_ref=dst, send_sem=send, recv_sem=recv, device_id=who, device_id_type=MESH
        )

    def ring(way, piece, d):
        if way == 0:
            a, b, who = d - 1, d, device(y, z + 1, t)
        else:
            a, b, who = lax.rem(17 - d, 16), 16 - d, device(y, z - 1, t)
        n = piece % (RP // 2)
        if piece < RP // 2:
            buf, part = kk, pl.ds(n * (512 // RP), 512 // RP)
        else:
            buf, part = vt, pl.ds(n * (256 // RP), 256 // RP)
        return remote(buf.at[a, part], buf.at[b, part], ring_s.at[piece // (RP // 2)], ring_r.at[way, piece, d], who)

    loads[1].wait()
    vt[0] = jnp.transpose(pv_in[...].astype(F32)).astype(BF16)

    loads[0].wait()
    pl.semaphore_wait(barrier, len(partners))
    for piece in range(RP):
        for way in range(2):
            ring(way, piece, 1).start()

    loads[2].wait()
    col = jnp.transpose(jnp.broadcast_to(idx_in[...].astype(F32), (128, 128)))
    i = lax.broadcasted_iota(jnp.int32, (128, 128), 0) - h * 32
    row = lax.broadcasted_iota(jnp.int32, (128, 128), 1) // 4
    mine = jnp.sum(jnp.where(i == row, col, 0.0), axis=0, keepdims=True)
    rank = jnp.sum(jnp.where((col == mine) & (i >= 0) & (i < row), 1.0, 0.0), axis=0, keepdims=True)
    position = lax.rem(lax.broadcasted_iota(jnp.int32, (1, 128), 1), 4).astype(F32)
    slot_row = mine * 16.0 + rank * 4.0 + position
    one_hot = jnp.where(lax.broadcasted_iota(jnp.int32, (256, 128), 0).astype(F32) == slot_row, 1.0, 0.0).astype(BF16)

    for n in (3, 4, 5, 6):
        loads[n].wait()

    def rows_of(ref):
        return ref[...].astype(F32).reshape(128, ref.shape[2]).astype(BF16)

    qs[:, :, 0:1024] = dot(one_hot, rows_of(q_in), 1, 0).astype(BF16).reshape(4, 64, 1024)
    qs[:, :, 1024:1152] = dot(one_hot, rows_of(ck_in), 1, 0).astype(BF16).reshape(4, 64, 128)
    qs[:, :, 1152:1280] = dot(one_hot, rows_of(cv_in), 1, 0).astype(BF16).reshape(4, 64, 128)
    q_copies = []
    for d in (1, 2, 3):
        q_copies.append(
            remote(qs.at[lax.rem(y + d, 4)], rq.at[y], q_s.at[0], q_r.at[0], device(y + d, z, t))
        )
        q_copies[-1].start()
    rq[y] = qs[y]

    def begin(rel, _):
        at = pl.ds(pl.multiple_of(lax.rem(z_lo + rel, 4) * 16, 16), 16)
        for g in range(8):
            for source in range(4):
                qb[rel, pl.ds(g * 64 + source * 16, 16), :] = rq[source, at, g * 128 : (g + 1) * 128]
        keys = jnp.concatenate([rq[source, at, 1024:1152] for source in range(4)], axis=0)
        values = jnp.concatenate([rq[source, at, 1152:1280] for source in range(4)], axis=0)
        s = dot(keys, qb[rel], 1, 1)
        key_row = lax.broadcasted_iota(jnp.int32, (64, 512), 0)
        query_row = lax.rem(lax.broadcasted_iota(jnp.int32, (64, 512), 1), 64)
        seen = (key_row // 4 == query_row // 4) & (key_row <= query_row)
        s = jnp.where(seen, s, -1e30)
        peak = jnp.max(s, axis=0, keepdims=True)
        e = jnp.exp((s - peak) * SCALE)
        top[rel] = peak
        tot[rel] = jnp.sum(e, axis=0, keepdims=True)
        acc[rel] = dot(values, e.astype(BF16), 0, 0)
        return 0

    def attend(k):
        rel = lax.rem(16 - k, 4)
        source = lax.rem(z - k + 16, 16)
        valid = lens[y * 4 + lax.rem(source, 4)] - 256 * (source // 4)
        s = dot(kk[k], qb[rel], 1, 1)
        s = jnp.where(lax.broadcasted_iota(jnp.int32, (256, 512), 0) < valid, s, -1e30)
        before = top[rel]
        peak = jnp.maximum(before, jnp.max(s, axis=0, keepdims=True))
        e = jnp.exp((s - peak) * SCALE)
        fade = jnp.exp((before - peak) * SCALE)
        top[rel] = peak
        tot[rel] = tot[rel] * fade + jnp.sum(e, axis=0, keepdims=True)
        acc[rel] = acc[rel] * fade + dot(vt[k], e.astype(BF16), 1, 0)

    def forward(d, half):
        for piece in range(half * RP // 2, (half + 1) * RP // 2):
            for way in range(2):
                ring(way, piece, d).wait_recv()
                if (piece < RP // 2) == (way == 0):
                    ring(way, piece, d + 1).start()
                else:
                    pl.when(d < 7)(ring(way, piece, d + 1).start)

    def pair(d, _):
        def both(j, _):
            attend(jnp.where(j == 0, d, 16 - d))
            return 0

        return lax.fori_loop(0, 2, both, 0)

    def step(d, _):
        forward(d, 0)
        attend(d - 2)
        forward(d, 1)
        attend(18 - d)
        return 0

    forward(1, 0)
    forward(1, 1)
    plane = jnp.floor(mine * 0.25)
    column_of = plane * 16.0 + rank * 4.0 + position
    below = mine - plane * 4.0
    for rel in range(4):
        here = lax.rem(z_lo + rel, 4).astype(F32)
        hit = (lax.broadcasted_iota(jnp.int32, (64, 128), 0).astype(F32) == column_of) & (below == here)
        oht[rel] = jnp.transpose(jnp.where(hit, 1.0, 0.0)).astype(BF16)
    forward(2, 0)
    forward(2, 1)
    remote(rq.at[0:3], rq.at[0:3], q_s.at[0], q_r.at[0], device(y, z, t)).wait_recv()
    lax.fori_loop(0, 4, begin, 0)
    attend(0)
    lax.fori_loop(3, 8, step, 0)
    lax.fori_loop(6, 8, pair, 0)

    def hand_back(d, rel, at):
        return remote(
            rs.at[lax.rem(y + d, 4), at], rr.at[y, at], ret_s.at[0], ret_r.at[rel], device(y + d, z, t)
        )

    def slot_rows(rel):
        return pl.ds(pl.multiple_of(lax.rem(z_lo + rel, 4) * 16, 16), 16)

    def finish(rel, _):
        at = slot_rows(rel)
        o = jnp.transpose(acc[rel] / tot[rel]).astype(BF16)
        for source in range(4):
            for g in range(8):
                lo = g * 64 + source * 16
                rs[source, at, g * 128 : (g + 1) * 128] = o[lo : lo + 16, :]
        for d in (1, 2, 3):
            hand_back(d, rel, at).start()
        rr[y, at, :] = rs[y, at, :]
        return 0

    lax.fori_loop(1, 4, finish, 0)
    for piece in range(RP):
        ring(0 if piece < RP // 2 else 1, piece, 8).wait_recv()
    attend(8)
    finish(0, 0)
    def spread(way, piece):
        up, rows = way % 2 == 0, 128 // AP
        if way < 2:
            src, dst, part = 0, 1 if up else 3, pl.ds(piece * rows, rows)
        else:
            src, dst = 1 if up else 3, 2
            part = pl.ds(piece * rows + (0 if up else rows // 2), rows // 2)
        who = device(y, z + 4 if up else z - 4, t)
        return remote(att.at[src, part], att.at[dst, part], ag_s.at[0], ag_r.at[way, piece], who)

    def returned(rel):
        some = rr.at[0:3, slot_rows(rel)]
        remote(some, some, ret_s.at[0], ret_r.at[rel], device(y, z, t)).wait_recv()
        return jnp.concatenate([rr[source, slot_rows(rel), :] for source in range(4)], axis=0)

    def unpack(rel, _):
        part_sum[...] += dot(oht[rel], returned(rel), 1, 0)
        return 0

    part_sum[...] = dot(oht[1], returned(1), 1, 0)
    lax.fori_loop(2, 4, unpack, 0)
    last = returned(0)
    rows = 128 // AP
    for piece in range(AP):
        at = slice(piece * rows, (piece + 1) * rows)
        att[0, at] = (part_sum[at] + dot(oht[0, at], last, 1, 0)).astype(BF16)
        for way in range(2):
            spread(way, piece).start()

    loads[7].wait()

    def share(d, number, at):
        return remote(ps.at[d, at], pr.at[d, at], p_s.at[0], p_r.at[number], device(y, z, t + d))

    def project(a, number, at):
        def column(d, _):
            cols = pl.ds(pl.multiple_of(lax.rem(t + d, 8) * 256, 256), 256)
            part = dot(a, w[:, cols], 1, 0).astype(BF16)

            @pl.when(d < 8)
            def _():
                ps[d, at, :] = part
                share(d, number, at).start()

            @pl.when(d == 8)
            def _():
                pr[0, at, :] = part

            return 0

        lax.fori_loop(1, 9, column, 0)

    spans = [pl.ds(0, 128)]
    project(att[0], 0, spans[0])
    for piece in range(AP):
        for way in range(2):
            spread(way, piece).wait_recv()
            spread(way + 2, piece).start()
        spans.append(pl.ds(128 + piece * 2 * rows, 2 * rows))
        lo = piece * rows
        project(jnp.concatenate([att[1, lo : lo + rows], att[3, lo : lo + rows]], axis=0), 1 + piece, spans[-1])

    def result(number, at, pieces):
        others = pr.at[1:8, at]
        remote(others, others, p_s.at[0], p_r.at[number], device(y, z, t)).wait_recv()
        total = pr[0, at, :].astype(F32)
        for d in range(1, 8):
            total = total + pr[d, at, :].astype(F32)
        for below, lo, first, count in pieces:
            home = lax.rem(h - below + 4, 4) * 32 + first // 4
            part = total[lo : lo + count].reshape(count // 4, 4, 256)
            out_ref[pl.ds(home, count // 4)] = part.astype(BF16)

    def near(piece):
        result(1 + piece, spans[1 + piece], [(1, 0, piece * rows, rows), (3, rows, piece * rows, rows)])

    def far(piece):
        result(1 + AP + piece, spans[1 + AP + piece], [(2, 0, piece * rows, rows)])

    for piece in range(AP):
        for way in range(2):
            spread(way + 2, piece).wait_recv()
        spans.append(pl.ds(384 + piece * rows, rows))
        project(att[2, piece * rows : (piece + 1) * rows], 1 + AP + piece, spans[-1])
    result(0, spans[0], [(0, 0, 0, 128)])
    for piece in range(AP):
        near(piece)
    for piece in range(AP):
        far(piece)

    for ref, sem in (
        (kk.at[0:15], ring_s.at[0]),
        (vt.at[0:15], ring_s.at[1]),
        (qs.at[0:3], q_s.at[0]),
        (rs.at[0:3], ret_s.at[0]),
        (att.at[0:3], ag_s.at[0]),
        (ps.at[1:8], p_s.at[0]),
    ):
        remote(ref, ref, sem, p_r.at[0], device(y, z, t)).wait_send()


def local(q, ck, cv, pk, pv, index, lens, w):
    dma = pltpu.SemaphoreType.DMA
    hbm = pl.BlockSpec(memory_space=pltpu.HBM)
    return pl.pallas_call(
        kernel,
        out_shape=pltpu.VMEM((128, 4, 256), BF16),
        in_specs=[hbm] * 8,
        out_specs=pl.BlockSpec(memory_space=pltpu.VMEM),
        scratch_shapes=[
            pltpu.SMEM((16,), jnp.int32),
            pltpu.VMEM((32, 4, 1024), BF16),
            pltpu.VMEM((32, 4, 128), BF16),
            pltpu.VMEM((32, 4, 128), BF16),
            pltpu.VMEM((256, 128), BF16),
            pltpu.VMEM((1, 128), jnp.int32),
            pltpu.VMEM((1024, 2048), BF16),
            pltpu.VMEM((16, 256, 128), BF16),
            pltpu.VMEM((16, 128, 256), BF16),
            pltpu.VMEM((4, 64, 1280), BF16),
            pltpu.VMEM((4, 64, 1280), BF16),
            pltpu.VMEM((4, 512, 128), BF16),
            pltpu.VMEM((4, 1, 512), F32),
            pltpu.VMEM((4, 1, 512), F32),
            pltpu.VMEM((4, 128, 512), F32),
            pltpu.VMEM((4, 64, 1024), BF16),
            pltpu.VMEM((4, 64, 1024), BF16),
            pltpu.VMEM((4, 128, 64), BF16),
            pltpu.VMEM((128, 1024), F32),
            pltpu.VMEM((4, 128, 1024), BF16),
            pltpu.VMEM((8, 512, 256), BF16),
            pltpu.VMEM((8, 512, 256), BF16),
            dma((8,)),
            dma((2,)),
            dma((2, RP, 9)),
            dma((1,)),
            dma((1,)),
            dma((1,)),
            dma((4,)),
            dma((1,)),
            dma((4, AP)),
            dma((1,)),
            dma((1 + 2 * AP,)),
        ],
        compiler_params=pltpu.CompilerParams(
            collective_id=0, has_side_effects=True, vmem_limit_bytes=56 * 1024 * 1024
        ),
    )(q, ck, cv, pk, pv, index.reshape(1, 128), lens, w)


def solution(mesh):
    return jax.shard_map(
        local,
        mesh=mesh,
        in_specs=(
            P(("group", "rows"), None, "tensor"),
            P(("group", "rows"), None, "tensor"),
            P(("group", "rows"), None, "tensor"),
            P("group", "rows", "tensor"),
            P("group", "rows", "tensor"),
            P("group", None),
            P(),
            P("tensor", "rows"),
        ),
        out_specs=P("group", None, ("rows", "tensor")),
        check_vma=False,
    )
```

```python
import functools
import math

import jax
import jax.numpy as jnp
from jax import lax
from jax.experimental import pallas as pl
from jax.experimental.pallas import tpu as pltpu
from jax.sharding import PartitionSpec as P

MESH = pl.DeviceIdType.MESH
SCALE = 1.0 / math.sqrt(128.0)
F32 = jnp.float32
BF16 = jnp.bfloat16
RP = 4
AP = 4


def place():
    g = lax.axis_index("group")
    return g // 4, lax.axis_index("rows") * 4 + lax.rem(g, 4), lax.axis_index("tensor")


def device(y, z, t):
    y, z, t = lax.rem(y + 4, 4), lax.rem(z + 16, 16), lax.rem(t + 8, 8)
    return (y * 4 + lax.rem(z, 4), z // 4, t)


def dot(a, b, da, db):
    return lax.dot_general(a, b, (((da,), (db,)), ((), ())), preferred_element_type=F32)


def kernel(
    q_hbm, ck_hbm, cv_hbm, pk_hbm, pv_hbm, idx_hbm, lens_hbm, w_hbm, out_ref,
    lens, q_in, ck_in, cv_in, pv_in, idx_in, w, kk, vt, qs, rq, qb, top, tot, acc, rs, rr, oht, part_sum, att, ps, pr,
    load_sem, ring_s, ring_r, q_s, q_r, ret_s, ret_r, ag_s, ag_r, p_s, p_r,
):
    y, z, t = place()
    z_lo, h = lax.rem(z, 4), z // 4

    barrier = pltpu.get_barrier_semaphore()
    partners = [device(y, z + d, t) for d in (1, -1, 4, -4)]
    partners += [device(y + d, z, t) for d in (1, 2, 3)]
    partners += [device(y, z, t + d) for d in range(1, 8)]
    for who in partners:
        pl.semaphore_signal(barrier, inc=1, device_id=who, device_id_type=MESH)

    loads = []
    for n, (src, dst) in enumerate(
        (
            (pk_hbm.at[0], kk.at[0]),
            (pv_hbm.at[0], pv_in),
            (idx_hbm, idx_in),
            (q_hbm, q_in),
            (ck_hbm, ck_in),
            (cv_hbm, cv_in),
            (lens_hbm, lens),
            (w_hbm, w),
        )
    ):
        loads.append(pltpu.make_async_copy(src, dst, load_sem.at[n]))
        loads[-1].start()

    def remote(src, dst, send, recv, who):
        return pltpu.make_async_remote_copy(
            src_ref=src, dst_ref=dst, send_sem=send, recv_sem=recv, device_id=who, device_id_type=MESH
        )

    def ring(way, piece, d):
        if way == 0:
            a, b, who = d - 1, d, device(y, z + 1, t)
        else:
            a, b, who = lax.rem(17 - d, 16), 16 - d, device(y, z - 1, t)
        n = piece % (RP // 2)
        if piece < RP // 2:
            buf, part = kk, pl.ds(n * (512 // RP), 512 // RP)
        else:
            buf, part = vt, pl.ds(n * (256 // RP), 256 // RP)
        return remote(buf.at[a, part], buf.at[b, part], ring_s.at[piece // (RP // 2)], ring_r.at[way, piece, d], who)

    loads[1].wait()
    vt[0] = jnp.transpose(pv_in[...].astype(F32)).astype(BF16)

    loads[0].wait()
    pl.semaphore_wait(barrier, len(partners))
    for piece in range(RP):
        for way in range(2):
            ring(way, piece, 1).start()

    loads[2].wait()
    col = jnp.transpose(jnp.broadcast_to(idx_in[...].astype(F32), (128, 128)))
    i = lax.broadcasted_iota(jnp.int32, (128, 128), 0) - h * 32
    row = lax.broadcasted_iota(jnp.int32, (128, 128), 1) // 4
    mine = jnp.sum(jnp.where(i == row, col, 0.0), axis=0, keepdims=True)
    rank = jnp.sum(jnp.where((col == mine) & (i >= 0) & (i < row), 1.0, 0.0), axis=0, keepdims=True)
    position = lax.rem(lax.broadcasted_iota(jnp.int32, (1, 128), 1), 4).astype(F32)
    slot_row = mine * 16.0 + rank * 4.0 + position
    one_hot = jnp.where(lax.broadcasted_iota(jnp.int32, (256, 128), 0).astype(F32) == slot_row, 1.0, 0.0).astype(BF16)

    for n in (3, 4, 5, 6):
        loads[n].wait()

    def rows_of(ref):
        return ref[...].astype(F32).reshape(128, ref.shape[2]).astype(BF16)

    qs[:, :, 0:1024] = dot(one_hot, rows_of(q_in), 1, 0).astype(BF16).reshape(4, 64, 1024)
    qs[:, :, 1024:1152] = dot(one_hot, rows_of(ck_in), 1, 0).astype(BF16).reshape(4, 64, 128)
    qs[:, :, 1152:1280] = dot(one_hot, rows_of(cv_in), 1, 0).astype(BF16).reshape(4, 64, 128)
    q_copies = []
    for d in (1, 2, 3):
        q_copies.append(
            remote(qs.at[lax.rem(y + d, 4)], rq.at[y], q_s.at[0], q_r.at[0], device(y + d, z, t))
        )
        q_copies[-1].start()
    rq[y] = qs[y]

    def begin(rel, _):
        at = pl.ds(pl.multiple_of(lax.rem(z_lo + rel, 4) * 16, 16), 16)
        for g in range(8):
            for source in range(4):
                qb[rel, pl.ds(g * 64 + source * 16, 16), :] = rq[source, at, g * 128 : (g + 1) * 128]
        keys = jnp.concatenate([rq[source, at, 1024:1152] for source in range(4)], axis=0)
        values = jnp.concatenate([rq[source, at, 1152:1280] for source in range(4)], axis=0)
        s = dot(keys, qb[rel], 1, 1)
        key_row = lax.broadcasted_iota(jnp.int32, (64, 512), 0)
        query_row = lax.rem(lax.broadcasted_iota(jnp.int32, (64, 512), 1), 64)
        seen = (key_row // 4 == query_row // 4) & (key_row <= query_row)
        s = jnp.where(seen, s, -1e30)
        peak = jnp.max(s, axis=0, keepdims=True)
        e = jnp.exp((s - peak) * SCALE)
        top[rel] = peak
        tot[rel] = jnp.sum(e, axis=0, keepdims=True)
        acc[rel] = dot(values, e.astype(BF16), 0, 0)
        return 0

    def attend(k):
        rel = lax.rem(16 - k, 4)
        source = lax.rem(z - k + 16, 16)
        valid = lens[y * 4 + lax.rem(source, 4)] - 256 * (source // 4)
        s = dot(kk[k], qb[rel], 1, 1)
        s = jnp.where(lax.broadcasted_iota(jnp.int32, (256, 512), 0) < valid, s, -1e30)
        before = top[rel]
        peak = jnp.maximum(before, jnp.max(s, axis=0, keepdims=True))
        e = jnp.exp((s - peak) * SCALE)
        fade = jnp.exp((before - peak) * SCALE)
        top[rel] = peak
        tot[rel] = tot[rel] * fade + jnp.sum(e, axis=0, keepdims=True)
        acc[rel] = acc[rel] * fade + dot(vt[k], e.astype(BF16), 1, 0)

    def forward(d, half):
        for piece in range(half * RP // 2, (half + 1) * RP // 2):
            for way in range(2):
                ring(way, piece, d).wait_recv()
                if (piece < RP // 2) == (way == 0):
                    ring(way, piece, d + 1).start()
                else:
                    pl.when(d < 7)(ring(way, piece, d + 1).start)

    def next_chunk(n):
        attend(jnp.where(n % 2 == 1, (n + 1) // 2, lax.rem(16 - n // 2, 16)))

    def step(d, _):
        forward(d, 0)
        next_chunk(3 * d - 9)
        forward(d, 1)
        next_chunk(3 * d - 8)
        next_chunk(3 * d - 7)
        return 0

    forward(1, 0)
    forward(1, 1)
    plane = jnp.floor(mine * 0.25)
    column_of = plane * 16.0 + rank * 4.0 + position
    below = mine - plane * 4.0
    for rel in range(4):
        here = lax.rem(z_lo + rel, 4).astype(F32)
        hit = (lax.broadcasted_iota(jnp.int32, (64, 128), 0).astype(F32) == column_of) & (below == here)
        oht[rel] = jnp.transpose(jnp.where(hit, 1.0, 0.0)).astype(BF16)
    forward(2, 0)
    forward(2, 1)
    remote(rq.at[0:3], rq.at[0:3], q_s.at[0], q_r.at[0], device(y, z, t)).wait_recv()
    lax.fori_loop(0, 4, begin, 0)
    lax.fori_loop(3, 8, step, 0)

    def hand_back(d, rel, at):
        return remote(
            rs.at[lax.rem(y + d, 4), at], rr.at[y, at], ret_s.at[0], ret_r.at[rel], device(y + d, z, t)
        )

    def slot_rows(rel):
        return pl.ds(pl.multiple_of(lax.rem(z_lo + rel, 4) * 16, 16), 16)

    def finish(rel, _):
        at = slot_rows(rel)
        o = jnp.transpose(acc[rel] / tot[rel]).astype(BF16)
        for source in range(4):
            for g in range(8):
                lo = g * 64 + source * 16
                rs[source, at, g * 128 : (g + 1) * 128] = o[lo : lo + 16, :]
        for d in (1, 2, 3):
            hand_back(d, rel, at).start()
        rr[y, at, :] = rs[y, at, :]
        return 0

    lax.fori_loop(1, 4, finish, 0)
    for piece in range(RP):
        ring(0 if piece < RP // 2 else 1, piece, 8).wait_recv()
    attend(8)
    finish(0, 0)
    def spread(way, piece):
        up, rows = way % 2 == 0, 128 // AP
        if way < 2:
            src, dst, part = 0, 1 if up else 3, pl.ds(piece * rows, rows)
        else:
            src, dst = 1 if up else 3, 2
            part = pl.ds(piece * rows + (0 if up else rows // 2), rows // 2)
        who = device(y, z + 4 if up else z - 4, t)
        return remote(att.at[src, part], att.at[dst, part], ag_s.at[0], ag_r.at[way, piece], who)

    def returned(rel):
        some = rr.at[0:3, slot_rows(rel)]
        remote(some, some, ret_s.at[0], ret_r.at[rel], device(y, z, t)).wait_recv()
        return jnp.concatenate([rr[source, slot_rows(rel), :] for source in range(4)], axis=0)

    def unpack(rel, _):
        part_sum[...] += dot(oht[rel], returned(rel), 1, 0)
        return 0

    part_sum[...] = dot(oht[1], returned(1), 1, 0)
    lax.fori_loop(2, 4, unpack, 0)
    last = returned(0)
    rows = 128 // AP
    for piece in range(AP):
        at = slice(piece * rows, (piece + 1) * rows)
        att[0, at] = (part_sum[at] + dot(oht[0, at], last, 1, 0)).astype(BF16)
        for way in range(2):
            spread(way, piece).start()

    loads[7].wait()

    def share(d, number, at):
        return remote(ps.at[d, at], pr.at[d, at], p_s.at[0], p_r.at[number], device(y, z, t + d))

    def project(a, number, at):
        def column(n, _):
            d = 4 + jnp.where(n % 2 == 0, n // 2, -((n + 1) // 2))
            cols = pl.ds(pl.multiple_of(lax.rem(t + d, 8) * 256, 256), 256)
            part = dot(a, w[:, cols], 1, 0).astype(BF16)

            @pl.when(d > 0)
            def _():
                ps[d, at, :] = part
                share(d, number, at).start()

            @pl.when(d == 0)
            def _():
                pr[0, at, :] = part

            return 0

        lax.fori_loop(0, 8, column, 0)

    spans = [pl.ds(0, 128)]
    project(att[0], 0, spans[0])
    for piece in range(AP):
        for way in range(2):
            spread(way, piece).wait_recv()
            spread(way + 2, piece).start()
        spans.append(pl.ds(128 + piece * 2 * rows, 2 * rows))
        lo = piece * rows
        project(jnp.concatenate([att[1, lo : lo + rows], att[3, lo : lo + rows]], axis=0), 1 + piece, spans[-1])

    def result(number, at, pieces):
        others = pr.at[1:8, at]
        remote(others, others, p_s.at[0], p_r.at[number], device(y, z, t)).wait_recv()
        total = pr[0, at, :].astype(F32)
        for d in range(1, 8):
            total = total + pr[d, at, :].astype(F32)
        for below, lo, first, count in pieces:
            home = lax.rem(h - below + 4, 4) * 32 + first // 4
            part = total[lo : lo + count].reshape(count // 4, 4, 256)
            out_ref[pl.ds(home, count // 4)] = part.astype(BF16)

    def near(piece):
        result(1 + piece, spans[1 + piece], [(1, 0, piece * rows, rows), (3, rows, piece * rows, rows)])

    def far(piece):
        result(1 + AP + piece, spans[1 + AP + piece], [(2, 0, piece * rows, rows)])

    for piece in range(AP):
        for way in range(2):
            spread(way + 2, piece).wait_recv()
        spans.append(pl.ds(384 + piece * rows, rows))
        project(att[2, piece * rows : (piece + 1) * rows], 1 + AP + piece, spans[-1])
    result(0, spans[0], [(0, 0, 0, 128)])
    for piece in range(AP):
        near(piece)
    for piece in range(AP):
        far(piece)

    for ref, sem in (
        (kk.at[0:15], ring_s.at[0]),
        (vt.at[0:15], ring_s.at[1]),
        (qs.at[0:3], q_s.at[0]),
        (rs.at[0:3], ret_s.at[0]),
        (att.at[0:3], ag_s.at[0]),
        (ps.at[1:8], p_s.at[0]),
    ):
        remote(ref, ref, sem, p_r.at[0], device(y, z, t)).wait_send()


def local(q, ck, cv, pk, pv, index, lens, w):
    dma = pltpu.SemaphoreType.DMA
    hbm = pl.BlockSpec(memory_space=pltpu.HBM)
    return pl.pallas_call(
        kernel,
        out_shape=pltpu.VMEM((128, 4, 256), BF16),
        in_specs=[hbm] * 8,
        out_specs=pl.BlockSpec(memory_space=pltpu.VMEM),
        scratch_shapes=[
            pltpu.SMEM((16,), jnp.int32),
            pltpu.VMEM((32, 4, 1024), BF16),
            pltpu.VMEM((32, 4, 128), BF16),
            pltpu.VMEM((32, 4, 128), BF16),
            pltpu.VMEM((256, 128), BF16),
            pltpu.VMEM((1, 128), jnp.int32),
            pltpu.VMEM((1024, 2048), BF16),
            pltpu.VMEM((16, 256, 128), BF16),
            pltpu.VMEM((16, 128, 256), BF16),
            pltpu.VMEM((4, 64, 1280), BF16),
            pltpu.VMEM((4, 64, 1280), BF16),
            pltpu.VMEM((4, 512, 128), BF16),
            pltpu.VMEM((4, 1, 512), F32),
            pltpu.VMEM((4, 1, 512), F32),
            pltpu.VMEM((4, 128, 512), F32),
            pltpu.VMEM((4, 64, 1024), BF16),
            pltpu.VMEM((4, 64, 1024), BF16),
            pltpu.VMEM((4, 128, 64), BF16),
            pltpu.VMEM((128, 1024), F32),
            pltpu.VMEM((4, 128, 1024), BF16),
            pltpu.VMEM((8, 512, 256), BF16),
            pltpu.VMEM((8, 512, 256), BF16),
            dma((8,)),
            dma((2,)),
            dma((2, RP, 9)),
            dma((1,)),
            dma((1,)),
            dma((1,)),
            dma((4,)),
            dma((1,)),
            dma((4, AP)),
            dma((1,)),
            dma((1 + 2 * AP,)),
        ],
        compiler_params=pltpu.CompilerParams(
            collective_id=0, has_side_effects=True, vmem_limit_bytes=56 * 1024 * 1024
        ),
    )(q, ck, cv, pk, pv, index.reshape(1, 128), lens, w)


def solution(mesh):
    return jax.shard_map(
        local,
        mesh=mesh,
        in_specs=(
            P(("group", "rows"), None, "tensor"),
            P(("group", "rows"), None, "tensor"),
            P(("group", "rows"), None, "tensor"),
            P("group", "rows", "tensor"),
            P("group", "rows", "tensor"),
            P("group", None),
            P(),
            P("tensor", "rows"),
        ),
        out_specs=P("group", None, ("rows", "tensor")),
        check_vma=False,
    )
```

```python
import functools
import math

import jax
import jax.numpy as jnp
from jax import lax
from jax.experimental import pallas as pl
from jax.experimental.pallas import tpu as pltpu
from jax.sharding import PartitionSpec as P

MESH = pl.DeviceIdType.MESH
SCALE = 1.0 / math.sqrt(128.0)
F32 = jnp.float32
BF16 = jnp.bfloat16
RP = 4
AP = 4


def place():
    g = lax.axis_index("group")
    return g // 4, lax.axis_index("rows") * 4 + lax.rem(g, 4), lax.axis_index("tensor")


def device(y, z, t):
    y, z, t = lax.rem(y + 4, 4), lax.rem(z + 16, 16), lax.rem(t + 8, 8)
    return (y * 4 + lax.rem(z, 4), z // 4, t)


def dot(a, b, da, db):
    return lax.dot_general(a, b, (((da,), (db,)), ((), ())), preferred_element_type=F32)


def kernel(
    q_hbm, ck_hbm, cv_hbm, pk_hbm, pv_hbm, idx_hbm, lens_hbm, w_hbm, out_ref,
    lens, q_in, ck_in, cv_in, pv_in, idx_in, w, kk, vt, qs, rq, qb, top, tot, acc, rs, rr, oht, part_sum, att, ps, pr,
    load_sem, ring_s, ring_r, q_s, q_r, ret_s, ret_r, ag_s, ag_r, p_s, p_r,
):
    y, z, t = place()
    z_lo, h = lax.rem(z, 4), z // 4

    barrier = pltpu.get_barrier_semaphore()
    partners = [device(y, z + d, t) for d in (1, -1, 4, -4)]
    partners += [device(y + d, z, t) for d in (1, 2, 3)]
    partners += [device(y, z, t + d) for d in range(1, 8)]
    for who in partners:
        pl.semaphore_signal(barrier, inc=1, device_id=who, device_id_type=MESH)

    loads = []
    for n, (src, dst) in enumerate(
        (
            (pk_hbm.at[0], kk.at[0]),
            (pv_hbm.at[0], pv_in),
            (idx_hbm, idx_in),
            (q_hbm, q_in),
            (ck_hbm, ck_in),
            (cv_hbm, cv_in),
            (lens_hbm, lens),
            (w_hbm, w),
        )
    ):
        loads.append(pltpu.make_async_copy(src, dst, load_sem.at[n]))
        loads[-1].start()

    def remote(src, dst, send, recv, who):
        return pltpu.make_async_remote_copy(
            src_ref=src, dst_ref=dst, send_sem=send, recv_sem=recv, device_id=who, device_id_type=MESH
        )

    def ring(way, piece, d):
        if way == 0:
            a, b, who = d - 1, d, device(y, z + 1, t)
        else:
            a, b, who = lax.rem(17 - d, 16), 16 - d, device(y, z - 1, t)
        n = piece % (RP // 2)
        if piece < RP // 2:
            buf, part = kk, pl.ds(n * (512 // RP), 512 // RP)
        else:
            buf, part = vt, pl.ds(n * (256 // RP), 256 // RP)
        return remote(buf.at[a, part], buf.at[b, part], ring_s.at[piece // (RP // 2)], ring_r.at[way, piece, d], who)

    loads[1].wait()
    vt[0] = jnp.transpose(pv_in[...].astype(F32)).astype(BF16)

    loads[0].wait()
    pl.semaphore_wait(barrier, len(partners))
    for piece in range(RP):
        for way in range(2):
            ring(way, piece, 1).start()

    loads[2].wait()
    col = jnp.transpose(jnp.broadcast_to(idx_in[...].astype(F32), (128, 128)))
    i = lax.broadcasted_iota(jnp.int32, (128, 128), 0) - h * 32
    row = lax.broadcasted_iota(jnp.int32, (128, 128), 1) // 4
    mine = jnp.sum(jnp.where(i == row, col, 0.0), axis=0, keepdims=True)
    rank = jnp.sum(jnp.where((col == mine) & (i >= 0) & (i < row), 1.0, 0.0), axis=0, keepdims=True)
    position = lax.rem(lax.broadcasted_iota(jnp.int32, (1, 128), 1), 4).astype(F32)
    slot_row = mine * 16.0 + rank * 4.0 + position
    one_hot = jnp.where(lax.broadcasted_iota(jnp.int32, (256, 128), 0).astype(F32) == slot_row, 1.0, 0.0).astype(BF16)

    for n in (3, 4, 5, 6):
        loads[n].wait()

    def rows_of(ref):
        return ref[...].astype(F32).reshape(128, ref.shape[2]).astype(BF16)

    qs[:, :, 0:1024] = dot(one_hot, rows_of(q_in), 1, 0).astype(BF16).reshape(4, 64, 1024)
    qs[:, :, 1024:1152] = dot(one_hot, rows_of(ck_in), 1, 0).astype(BF16).reshape(4, 64, 128)
    qs[:, :, 1152:1280] = dot(one_hot, rows_of(cv_in), 1, 0).astype(BF16).reshape(4, 64, 128)
    q_copies = []
    for d in (1, 2, 3):
        q_copies.append(
            remote(qs.at[lax.rem(y + d, 4)], rq.at[y], q_s.at[0], q_r.at[0], device(y + d, z, t))
        )
        q_copies[-1].start()
    rq[y] = qs[y]

    def begin(rel, _):
        at = pl.ds(pl.multiple_of(lax.rem(z_lo + rel, 4) * 16, 16), 16)
        for g in range(8):
            for source in range(4):
                qb[rel, pl.ds(g * 64 + source * 16, 16), :] = rq[source, at, g * 128 : (g + 1) * 128]
        keys = jnp.concatenate([rq[source, at, 1024:1152] for source in range(4)], axis=0)
        values = jnp.concatenate([rq[source, at, 1152:1280] for source in range(4)], axis=0)
        s = dot(keys, qb[rel], 1, 1)
        key_row = lax.broadcasted_iota(jnp.int32, (64, 512), 0)
        query_row = lax.rem(lax.broadcasted_iota(jnp.int32, (64, 512), 1), 64)
        seen = (key_row // 4 == query_row // 4) & (key_row <= query_row)
        s = jnp.where(seen, s, -1e30)
        peak = jnp.max(s, axis=0, keepdims=True)
        e = jnp.exp((s - peak) * SCALE)
        top[rel] = peak
        tot[rel] = jnp.sum(e, axis=0, keepdims=True)
        acc[rel] = dot(values, e.astype(BF16), 0, 0)
        return 0

    def attend(k):
        rel = lax.rem(16 - k, 4)
        source = lax.rem(z - k + 16, 16)
        valid = lens[y * 4 + lax.rem(source, 4)] - 256 * (source // 4)
        s = dot(kk[k], qb[rel], 1, 1)
        s = jnp.where(lax.broadcasted_iota(jnp.int32, (256, 512), 0) < valid, s, -1e30)
        before = top[rel]
        peak = jnp.maximum(before, jnp.max(s, axis=0, keepdims=True))
        e = jnp.exp((s - peak) * SCALE)
        fade = jnp.exp((before - peak) * SCALE)
        top[rel] = peak
        tot[rel] = tot[rel] * fade + jnp.sum(e, axis=0, keepdims=True)
        acc[rel] = acc[rel] * fade + dot(vt[k], e.astype(BF16), 1, 0)

    def forward(d, half):
        for piece in range(half * RP // 2, (half + 1) * RP // 2):
            for way in range(2):
                ring(way, piece, d).wait_recv()
                if (piece < RP // 2) == (way == 0):
                    ring(way, piece, d + 1).start()
                else:
                    pl.when(d < 7)(ring(way, piece, d + 1).start)

    def next_chunk(n):
        attend(jnp.where(n % 2 == 1, (n + 1) // 2, lax.rem(16 - n // 2, 16)))

    def step(d, _):
        forward(d, 0)
        next_chunk(3 * d - 9)
        forward(d, 1)
        next_chunk(3 * d - 8)
        next_chunk(3 * d - 7)
        return 0

    lax.fori_loop(1, 3, lambda d, _: forward(d, 0) or forward(d, 1) or 0, 0)
    plane = jnp.floor(mine * 0.25)
    column_of = plane * 16.0 + rank * 4.0 + position
    below = mine - plane * 4.0
    for rel in range(4):
        here = lax.rem(z_lo + rel, 4).astype(F32)
        hit = (lax.broadcasted_iota(jnp.int32, (64, 128), 0).astype(F32) == column_of) & (below == here)
        oht[rel] = jnp.transpose(jnp.where(hit, 1.0, 0.0)).astype(BF16)
    remote(rq.at[0:3], rq.at[0:3], q_s.at[0], q_r.at[0], device(y, z, t)).wait_recv()
    lax.fori_loop(0, 4, begin, 0)
    lax.fori_loop(3, 8, step, 0)

    def hand_back(d, rel, at):
        return remote(
            rs.at[lax.rem(y + d, 4), at], rr.at[y, at], ret_s.at[0], ret_r.at[rel], device(y + d, z, t)
        )

    def slot_rows(rel):
        return pl.ds(pl.multiple_of(lax.rem(z_lo + rel, 4) * 16, 16), 16)

    def finish(rel, _):
        at = slot_rows(rel)
        o = jnp.transpose(acc[rel] / tot[rel]).astype(BF16)
        for source in range(4):
            for g in range(8):
                lo = g * 64 + source * 16
                rs[source, at, g * 128 : (g + 1) * 128] = o[lo : lo + 16, :]
        for d in (2, 1, 3):
            hand_back(d, rel, at).start()
        rr[y, at, :] = rs[y, at, :]
        return 0

    lax.fori_loop(1, 4, finish, 0)
    for piece in range(RP):
        ring(0 if piece < RP // 2 else 1, piece, 8).wait_recv()
    attend(8)
    finish(0, 0)
    def spread(way, piece):
        up, rows = way % 2 == 0, 128 // AP
        if way < 2:
            src, dst, part = 0, 1 if up else 3, pl.ds(piece * rows, rows)
        else:
            src, dst = 1 if up else 3, 2
            part = pl.ds(piece * rows + (0 if up else rows // 2), rows // 2)
        who = device(y, z + 4 if up else z - 4, t)
        return remote(att.at[src, part], att.at[dst, part], ag_s.at[0], ag_r.at[way, piece], who)

    def returned(rel):
        some = rr.at[0:3, slot_rows(rel)]
        remote(some, some, ret_s.at[0], ret_r.at[rel], device(y, z, t)).wait_recv()
        return jnp.concatenate([rr[source, slot_rows(rel), :] for source in range(4)], axis=0)

    def unpack(rel, _):
        part_sum[...] += dot(oht[rel], returned(rel), 1, 0)
        return 0

    part_sum[...] = dot(oht[1], returned(1), 1, 0)
    lax.fori_loop(2, 4, unpack, 0)
    last = returned(0)
    rows = 128 // AP
    for piece in range(AP):
        at = slice(piece * rows, (piece + 1) * rows)
        att[0, at] = (part_sum[at] + dot(oht[0, at], last, 1, 0)).astype(BF16)
        for way in range(2):
            spread(way, piece).start()

    loads[7].wait()

    def share(d, number, at):
        return remote(ps.at[d, at], pr.at[d, at], p_s.at[0], p_r.at[number], device(y, z, t + d))

    def project(a, number, at):
        def column(n, _):
            d = 4 + jnp.where(n % 2 == 0, n // 2, -((n + 1) // 2))
            cols = pl.ds(pl.multiple_of(lax.rem(t + d, 8) * 256, 256), 256)
            part = dot(a, w[:, cols], 1, 0).astype(BF16)

            @pl.when(d > 0)
            def _():
                ps[d, at, :] = part
                share(d, number, at).start()

            @pl.when(d == 0)
            def _():
                pr[0, at, :] = part

            return 0

        lax.fori_loop(0, 8, column, 0)

    spans = [pl.ds(0, 128)]
    project(att[0], 0, spans[0])
    for piece in range(AP):
        for way in range(2):
            spread(way, piece).wait_recv()
            spread(way + 2, piece).start()
        spans.append(pl.ds(128 + piece * 2 * rows, 2 * rows))
        lo = piece * rows
        project(jnp.concatenate([att[1, lo : lo + rows], att[3, lo : lo + rows]], axis=0), 1 + piece, spans[-1])

    def result(number, at, pieces):
        others = pr.at[1:8, at]
        remote(others, others, p_s.at[0], p_r.at[number], device(y, z, t)).wait_recv()
        total = pr[0, at, :].astype(F32)
        for d in range(1, 8):
            total = total + pr[d, at, :].astype(F32)
        for below, lo, first, count in pieces:
            home = lax.rem(h - below + 4, 4) * 32 + first // 4
            part = total[lo : lo + count].reshape(count // 4, 4, 256)
            out_ref[pl.ds(home, count // 4)] = part.astype(BF16)

    def near(piece):
        result(1 + piece, spans[1 + piece], [(1, 0, piece * rows, rows), (3, rows, piece * rows, rows)])

    def far(piece):
        result(1 + AP + piece, spans[1 + AP + piece], [(2, 0, piece * rows, rows)])

    for piece in range(AP):
        for way in range(2):
            spread(way + 2, piece).wait_recv()
        spans.append(pl.ds(384 + piece * rows, rows))
        project(att[2, piece * rows : (piece + 1) * rows], 1 + AP + piece, spans[-1])
    result(0, spans[0], [(0, 0, 0, 128)])
    for piece in range(AP):
        near(piece)
    for piece in range(AP):
        far(piece)

    for ref, sem in (
        (kk.at[0:15], ring_s.at[0]),
        (vt.at[0:15], ring_s.at[1]),
        (qs.at[0:3], q_s.at[0]),
        (rs.at[0:3], ret_s.at[0]),
        (att.at[0:3], ag_s.at[0]),
        (ps.at[1:8], p_s.at[0]),
    ):
        remote(ref, ref, sem, p_r.at[0], device(y, z, t)).wait_send()


def local(q, ck, cv, pk, pv, index, lens, w):
    dma = pltpu.SemaphoreType.DMA
    hbm = pl.BlockSpec(memory_space=pltpu.HBM)
    return pl.pallas_call(
        kernel,
        out_shape=pltpu.VMEM((128, 4, 256), BF16),
        in_specs=[hbm] * 8,
        out_specs=pl.BlockSpec(memory_space=pltpu.VMEM),
        scratch_shapes=[
            pltpu.SMEM((16,), jnp.int32),
            pltpu.VMEM((32, 4, 1024), BF16),
            pltpu.VMEM((32, 4, 128), BF16),
            pltpu.VMEM((32, 4, 128), BF16),
            pltpu.VMEM((256, 128), BF16),
            pltpu.VMEM((1, 128), jnp.int32),
            pltpu.VMEM((1024, 2048), BF16),
            pltpu.VMEM((16, 256, 128), BF16),
            pltpu.VMEM((16, 128, 256), BF16),
            pltpu.VMEM((4, 64, 1280), BF16),
            pltpu.VMEM((4, 64, 1280), BF16),
            pltpu.VMEM((4, 512, 128), BF16),
            pltpu.VMEM((4, 1, 512), F32),
            pltpu.VMEM((4, 1, 512), F32),
            pltpu.VMEM((4, 128, 512), F32),
            pltpu.VMEM((4, 64, 1024), BF16),
            pltpu.VMEM((4, 64, 1024), BF16),
            pltpu.VMEM((4, 128, 64), BF16),
            pltpu.VMEM((128, 1024), F32),
            pltpu.VMEM((4, 128, 1024), BF16),
            pltpu.VMEM((8, 512, 256), BF16),
            pltpu.VMEM((8, 512, 256), BF16),
            dma((8,)),
            dma((2,)),
            dma((2, RP, 9)),
            dma((1,)),
            dma((1,)),
            dma((1,)),
            dma((4,)),
            dma((1,)),
            dma((4, AP)),
            dma((1,)),
            dma((1 + 2 * AP,)),
        ],
        compiler_params=pltpu.CompilerParams(
            collective_id=0, has_side_effects=True, vmem_limit_bytes=56 * 1024 * 1024
        ),
    )(q, ck, cv, pk, pv, index.reshape(1, 128), lens, w)


def solution(mesh):
    return jax.shard_map(
        local,
        mesh=mesh,
        in_specs=(
            P(("group", "rows"), None, "tensor"),
            P(("group", "rows"), None, "tensor"),
            P(("group", "rows"), None, "tensor"),
            P("group", "rows", "tensor"),
            P("group", "rows", "tensor"),
            P("group", None),
            P(),
            P("tensor", "rows"),
        ),
        out_specs=P("group", None, ("rows", "tensor")),
        check_vma=False,
    )
```
